32 devices in a mesh: sub: 8 (over z, y), fac: 4 (over x, core).
Axes of the slice: x: 2, y: 2, z: 4, core: 2. Of those that a mesh axis runs over, the one named last changes fastest.
Arguments:
- visibility: bfloat16 [12288, 256], P(('sub', 'fac')), may hold values from -6 to 6
- vis_weight: bfloat16 [12288, 128], P(('sub', 'fac')), may hold values from 0.099609375 to 1
- tap_start: int32 [12288, 2], P(('sub', 'fac')), may hold values from 4096 to 127999
- tap_step: int32 [12288, 2], P(('sub', 'fac')), may hold values from 102 to 818
- subgrid_id: int32 [12288], P(('sub', 'fac')), may hold values from 0 to 23, as said below
- w_plane: int32 [12288], P(('sub', 'fac')), may hold values from 0 to 3
- tile_intersection: int32 [24, 2], P('sub'), may hold values from 0 to 7936, as said below
Outputs:
- uv_planes: float32 [4, 2, 1024, 8192], P('fac', None, 'sub')
The draws below stay inside these ranges and needn't reach their ends.
Inputs may be any that keep to these rules, and one draw needn't show every extreme that they name: Within the rows of one device at most 8 rows name the same pair of subgrid_id and w_plane, and one pair is named by exactly 8 rows of every device. `tile_intersection`: column 0 is below 128; column 1 is at most 7936.
All inputs are finite; a program needn't handle non-finite values.
Results may differ from the reference program's by a relative error of at most 0.0038.
Values may be sent and summed in bfloat16 or wider, within the bound.
A program may use at most 64 MiB of HBM per device.

```python
import math
import jax
import jax.numpy as jnp
from jax import lax

C = 128
SG = 256
GS = 8192
BAND = 128
SG_DEV = 3
ROWS_DEV = 384
ROWS = 12288
NSG = 24
PLANES = 4
STRIP = 1024
CAP = 8


def route_draw(key):
    dest_count = NSG * PLANES
    blocks = ROWS // ROWS_DEV
    hottest = jax.random.randint(jax.random.fold_in(key, 11), (), 0, dest_count)
    block_keys = jax.random.split(jax.random.fold_in(key, 12), blocks)

    def one_block(block_key):
        key_pick, key_order = jax.random.split(block_key)
        remainder = CAP + jax.random.permutation(key_pick, dest_count * CAP - CAP)[:ROWS_DEV - CAP]
        chosen = jnp.concatenate([jnp.arange(CAP, dtype=jnp.int32), remainder.astype(jnp.int32)])
        target = (chosen // CAP + hottest) % dest_count
        return target[jax.random.permutation(key_order, ROWS_DEV)]
    return jax.vmap(one_block)(block_keys).reshape(ROWS).astype(jnp.int32)


def draw_subgrid_id(key, part):
    return route_draw(key) // PLANES


def draw_w_plane(key, part):
    return route_draw(key) % PLANES


def draw_tile_intersection(key, part):
    key_row, key_col = jax.random.split(jax.random.fold_in(key, 21))
    first_row = jax.random.randint(key_row, (NSG, 1), 0, BAND)
    first_col = jax.random.randint(key_col, (NSG, 1), 0, GS - SG + 1)
    return jnp.concatenate([first_row, first_col], axis=1).astype(jnp.int32)


def set_ends(array, own_key, least, top_value):
    shape = array.shape
    spot = [jax.random.randint(jax.random.fold_in(own_key, axis), (), 0, shape[axis]) for axis in range(len(shape))]
    array = array.at[tuple(spot)].set(least)
    longest = shape.index(max(shape))
    spot[longest] = (spot[longest] + 1) % shape[longest]
    return array.at[tuple(spot)].set(top_value)


def levels(own_key, shape, shards, least, largest):
    loudness, own = 1.0, jax.random.fold_in(own_key, 6)
    for dim, parts in shards:
        steps = jnp.exp(jax.random.uniform(jax.random.fold_in(own, dim), (parts,), jnp.float32, least / len(shards), largest / len(shards)))
        loudness = loudness * jnp.repeat(steps, shape[dim] // parts).reshape([-1 if axis == dim else 1 for axis in range(len(shape))])
    return loudness


def bell_draw(key, shape, deviation, most, shards=(), kind=jnp.bfloat16):
    values = deviation * jax.random.normal(key, shape, jnp.float32)
    if shards:
        values = values * levels(key, shape, shards, -0.22, 0.18)
    return jnp.clip(values, -most, most).astype(kind)


def setup_inputs(seed: int = 0) -> dict:
    seeds = jax.random.split(jax.random.key(seed), 8)
    return {
        "visibility": bell_draw(seeds[0], (ROWS, 2 * C), 1.0, 6.0, ((0, 32),)),
        "vis_weight": jnp.clip(jnp.exp(math.log(1.0) - 2.306499 * jax.random.uniform(seeds[1], (ROWS, C), jnp.float32) ** levels(seeds[1], (ROWS, C), ((0, 32),), -0.2, 0.2)), 0.099609375, 1.0).astype(jnp.bfloat16),
        "tap_start": set_ends(jax.random.randint(seeds[2], (ROWS, 2), 4 * 1024, (SG // 2 - 3) * 1024), jax.random.fold_in(seeds[2], 1), 4 * 1024, ((SG // 2 - 3) * 1024) - 1).astype(jnp.int32),
        "tap_step": set_ends(jax.random.randint(seeds[3], (ROWS, 2), SG * 1024 // (20 * C), 2 * SG * 1024 // (5 * C)), jax.random.fold_in(seeds[3], 1), SG * 1024 // (20 * C), (2 * SG * 1024 // (5 * C)) - 1).astype(jnp.int32),
        "subgrid_id": draw_subgrid_id(jax.random.fold_in(seeds[7], 71), 0),
        "w_plane": draw_w_plane(jax.random.fold_in(seeds[7], 71), 0),
        "tile_intersection": draw_tile_intersection(jax.random.fold_in(seeds[7], 71), 0),
    }


kernel_beta = 18.0
kernel_norm = 1.6e-07
fixed_unit = 1.0 / 1024.0

def bessel_zero(value):
    quarter = value * value * 0.25
    term = jnp.ones_like(value)
    total = jnp.ones_like(value)
    for order in range(1, 40):
        term = term * quarter * (1.0 / (order * order))
        total = total + term
    return total

def kaiser(offset):
    inside = jnp.maximum(1.0 - offset * offset * 0.0625, 0.0)
    return (bessel_zero(kernel_beta * jnp.sqrt(inside)) - 1.0) * kernel_norm

def track_positions(track, chans):
    channel = jnp.arange(chans, dtype=jnp.int32)
    along_u = track[:, 0:1] + channel[None, :] * track[:, 2:3]
    along_v = track[:, 1:2] + channel[None, :] * track[:, 3:4]
    return (along_u.astype(jnp.float32) * fixed_unit, along_v.astype(jnp.float32) * fixed_unit)

def kernel_taps(position):
    start = jnp.floor(position) - 3.0
    spread = jnp.arange(8, dtype=jnp.float32)
    return (kaiser(start[..., None] + spread - position[..., None]), start)

def reference(visibility, vis_weight, tap_start, tap_step, subgrid_id, w_plane, tile_intersection):
    chans = C
    block = math.gcd(ROWS, 128)
    count = ROWS // block
    which = (w_plane * NSG + subgrid_id).astype(jnp.int32)
    track = jnp.concatenate([tap_start, tap_step], axis=1)
    numbers = lax.ScatterDimensionNumbers(update_window_dims=(1,), inserted_window_dims=(0, 1, 2), scatter_dims_to_operand_dims=(0, 1, 2, 3))
    shape_four = (block, 2, chans, 8)

    def step(grids, pieces):
        vis_block, weight_block, track_block, which_block = pieces
        pos_u, pos_v = track_positions(track_block, chans)
        weights_u, start_u = kernel_taps(pos_u)
        weights_v, start_v = kernel_taps(pos_v)
        scaled = vis_block.astype(jnp.float32).reshape(block, 2, chans) * weight_block.astype(jnp.float32)[:, None, :]
        left = lax.optimization_barrier((scaled[..., None] * weights_v[:, None]).astype(jnp.bfloat16)).astype(jnp.float32)
        right = lax.optimization_barrier(weights_u.astype(jnp.bfloat16)).astype(jnp.float32)
        product = left[..., None] * right[:, None, :, None, :]
        grid_index = jnp.broadcast_to(which_block[:, None, None, None], shape_four)
        part_index = jnp.broadcast_to(jnp.arange(2, dtype=jnp.int32)[None, :, None, None], shape_four)
        row_index = jnp.broadcast_to(start_v.astype(jnp.int32)[:, None, :, None] + jnp.arange(8, dtype=jnp.int32)[None, None, None, :], shape_four)
        col_index = jnp.broadcast_to(start_u.astype(jnp.int32)[:, None, :, None], shape_four)
        indices = jnp.stack([grid_index, part_index, row_index, col_index], axis=-1).reshape(-1, 4)
        return (lax.scatter_add(grids, indices, product.reshape(-1, 8), numbers), None)
    pieces = (visibility.reshape(count, block, 2 * chans), vis_weight.reshape(count, block, chans), track.reshape(count, block, 4), which.reshape(count, block))
    grids, unused = lax.scan(step, jnp.zeros((PLANES * NSG, 2, SG, SG), jnp.float32), pieces)
    planes = grids.reshape(PLANES, NSG, 2, SG, SG)
    row_span = jnp.arange(SG, dtype=jnp.int32)
    zero = jnp.zeros((), jnp.int32)

    def place(index, image):
        position = jnp.asarray(index).astype(jnp.int32)
        tile = lax.dynamic_index_in_dim(planes, position, 1, keepdims=False)
        first = position // SG_DEV * BAND + tile_intersection[position, 0]
        column = tile_intersection[position, 1].astype(jnp.int32)
        slab = lax.dynamic_slice(image, (zero, zero, zero, column), (PLANES, 2, STRIP, SG))
        slab = slab.at[:, :, (first + row_span) % STRIP, :].add(tile)
        return lax.dynamic_update_slice(image, slab, (zero, zero, zero, column))
    return lax.fori_loop(0, NSG, place, jnp.zeros((PLANES, 2, STRIP, GS), jnp.float32))
```

```python
import functools
import math

import jax
import jax.numpy as jnp
from jax import lax
from jax.experimental import pallas as pl
from jax.experimental.pallas import tpu as pltpu
from jax.sharding import PartitionSpec as P

SG = 256
GS = 8192
BAND = 128
LANES = 128
BATCH = 8
VMEM_LIMIT = 48 * 1024 * 1024

kernel_norm = 1.6e-07
SERIES = [kernel_norm * 81.0**k / math.factorial(k) ** 2 for k in range(1, 40)]

NT = (((1,), (1,)), ((), ()))
NN = (((1,), (0,)), ((), ()))


def iota(shape, axis):
    return lax.broadcasted_iota(jnp.int32, shape, axis)


def onehot(mask):
    return jnp.where(mask, 1.0, 0.0).astype(jnp.bfloat16)


def dot(a, b, dims=NN):
    return lax.dot_general(a, b, dims, preferred_element_type=jnp.float32)


def pack_kernel(capacity, dest_count, target, vis, weight, start, step, packet):
    rows = vis.shape[0]
    slots = packet.shape[0]
    goal = target[...]
    named = iota((dest_count, rows), 0) == goal
    ahead = onehot(iota((rows, rows), 0) < iota((rows, rows), 1))
    before = dot(onehot(named), ahead)
    rank = jnp.sum(jnp.where(named, before, 0.0), axis=0, keepdims=True)
    slot = goal * capacity + rank.astype(jnp.int32)
    place = onehot(iota((slots, rows), 0) == slot)
    lane = iota((rows, LANES), 1)
    begin, pace = start[...], step[...]
    value = jnp.where(lane < 3, begin[:, 0:1], begin[:, 1:2])
    value = jnp.where(lane < 6, value, pace[:, 0:1])
    value = jnp.where(lane < 8, value, pace[:, 1:2])
    piece = jnp.where(lane < 3, lane, lane - 3)
    piece = jnp.where(lane < 6, piece, lane - 6)
    piece = jnp.where(lane < 8, piece, lane - 8)
    piece = jnp.minimum(piece, 3) * 8
    value = jnp.right_shift(value, piece) & 255
    value = jnp.where(lane < 10, value, jnp.where(lane == 10, 1, 0))
    track = value.astype(jnp.float32).astype(jnp.bfloat16)
    packet[:, 0 : 2 * LANES] = dot(place, vis[...]).astype(jnp.bfloat16)
    packet[:, 2 * LANES : 3 * LANES] = dot(place, weight[...]).astype(jnp.bfloat16)
    packet[:, 3 * LANES : 4 * LANES] = dot(place, track).astype(jnp.bfloat16)


def sort_kernel(capacity, members, packet, scaled, position, counts):
    slots = packet.shape[0]
    part = slots // members
    track = packet[:, 3 * LANES : 4 * LANES]
    used = dot(onehot(iota((8, LANES), 1) == 10), track, NT)[0:1]
    slot = iota((1, slots), 1).astype(jnp.float32)
    group = jnp.floor((slot + 0.5) * (1.0 / capacity))
    cycle = jnp.floor((group + 0.5) * (1.0 / members))
    member = (group - cycle * members).astype(jnp.int32)
    ahead = onehot(iota((slots, slots), 0) < iota((slots, slots), 1))
    mine = (iota((8, slots), 0) == member) & (used > 0.5)
    before = dot(onehot(mine), ahead)
    rank = jnp.sum(jnp.where(mine, before, 0.0), axis=0, keepdims=True).astype(jnp.int32)
    goal = jnp.where(used > 0.5, member * part + rank, -1)
    place = onehot(iota((slots, slots), 0) == goal)
    for m in range(members):
        counts[m] = jnp.sum(jnp.where((member == m) & (used > 0.5), 1, 0))
    weight = dot(place, packet[:, 2 * LANES : 3 * LANES])
    scaled[:, 0:LANES] = dot(place, packet[:, 0:LANES]) * weight
    scaled[:, LANES : 2 * LANES] = dot(place, packet[:, LANES : 2 * LANES]) * weight
    line, chan = iota((LANES, LANES), 0), iota((LANES, LANES), 1)
    moved = dot(place, track).astype(jnp.bfloat16)
    for axis in range(2):
        mix = jnp.zeros((LANES, LANES), jnp.int32)
        for n in range(3):
            mix = jnp.where(line == 3 * axis + n, 256**n, mix)
        for n in range(2):
            mix = jnp.where(line == 6 + 2 * axis + n, chan * 256**n, mix)
        mix = mix.astype(jnp.float32).astype(jnp.bfloat16)
        position[:, axis * LANES : (axis + 1) * LANES] = dot(moved, mix).astype(jnp.int32)


def taps(place):
    shape = (place.shape[0], 8, LANES)
    spot = jnp.broadcast_to(place[:, None, :], shape)
    first = jnp.right_shift(spot, 10) - 3
    cell = first + ((iota(shape, 1) - first) & 7)
    offset = (cell * 1024 - spot).astype(jnp.float32) * (1.0 / 1024.0)
    inside = jnp.maximum(1.0 - offset * offset * 0.0625, 0.0)
    total = jnp.full(shape, SERIES[-1], jnp.float32)
    for term in SERIES[-2::-1]:
        total = total * inside + term
    return total * inside, cell


def halves(cell):
    block = jnp.right_shift(cell, 4)
    upper = (cell & 8) != 0
    low = jnp.where(upper, -1, block)
    high = jnp.where(upper, block, -1)
    return jnp.concatenate([low, high], axis=1).astype(jnp.float32).astype(jnp.bfloat16)


def twice(value):
    return jnp.concatenate([value, value], axis=1).astype(jnp.bfloat16)


def grid_kernel(member, scaled, position, counts, corner, own, near, far, left, right, total):
    total[...] = jnp.zeros_like(total)

    def batch(b, carry):
        rows = pl.ds(pl.multiple_of(b * BATCH, BATCH), BATCH)
        tap_u, cell_u = taps(position[rows, 0:LANES])
        tap_v, cell_v = taps(position[rows, LANES : 2 * LANES])
        block_u, block_v = halves(cell_u), halves(cell_v)
        right_tap = twice(tap_u)
        real = twice(scaled[rows, 0:LANES][:, None, :] * tap_v)
        imag = twice(scaled[rows, LANES : 2 * LANES][:, None, :] * tap_v)
        zero = jnp.zeros((16, LANES), jnp.bfloat16)
        for r in range(BATCH):
            cols = slice(r * LANES, (r + 1) * LANES)
            for k in range(SG // 16):
                here = block_u[r] == k
                right[k * 16 : (k + 1) * 16, cols] = jnp.where(here, right_tap[r], zero)
                here = block_v[r] == k
                left[k * 16 : (k + 1) * 16, cols] = jnp.where(here, real[r], zero)
                left[SG + k * 16 : SG + (k + 1) * 16, cols] = jnp.where(here, imag[r], zero)
        total[...] += dot(left[...], right[...], NT)
        return carry

    lax.fori_loop(0, (counts[member] + BATCH - 1) // BATCH, batch, 0)
    shift = corner[member, 0]
    for p in range(2):
        grid = total[p * SG : (p + 1) * SG, :]
        spread = jnp.concatenate([grid, jnp.zeros((BAND, SG), jnp.float32)], axis=0)
        spread = pltpu.roll(spread, shift, 0)
        own[p] = spread[0:BAND]
        near[p] = spread[BAND : 2 * BAND].astype(near.dtype)
        far[p] = spread[2 * BAND :].astype(far.dtype)


def place_kernel(count, columns, *refs):
    band = refs[-1]
    width = band.shape[-1]
    band[...] = jnp.zeros_like(band)
    for n, ref in enumerate(refs[:-1]):
        column = columns[n]
        base = jnp.minimum(lax.shift_right_logical(column, 7), (width - 3 * LANES) // LANES)
        piece = ref[0].astype(jnp.float32)
        piece = jnp.concatenate([piece, jnp.zeros((piece.shape[0], LANES), jnp.float32)], axis=1)
        piece = pltpu.roll(piece, column - base * LANES, 1)
        cols = pl.ds(pl.multiple_of(base * LANES, LANES), 3 * LANES)
        band[0, 0, :, cols] += piece


def params(**extra):
    return pltpu.CompilerParams(vmem_limit_bytes=VMEM_LIMIT, **extra)


def whole(count):
    return [pl.BlockSpec(memory_space=pltpu.VMEM)] * count


def shards(visibility, vis_weight, tap_start, tap_step, subgrid_id, w_plane, tile_intersection):
    sub_count = lax.axis_size("sub")
    fac_count = lax.axis_size("fac")
    rows, chans = vis_weight.shape
    members = tile_intersection.shape[0]
    dest_count = sub_count * fac_count * members
    capacity = max(2, (2 * rows + dest_count - 1) // dest_count)
    slots = dest_count * capacity
    part = slots // members
    smem = pl.BlockSpec(memory_space=pltpu.SMEM)

    columns = tile_intersection[:, 1]
    ring = lambda d: [((i - d) % sub_count, i) for i in range(sub_count)]
    next_cols = lax.ppermute(columns, "sub", ring(1))
    far_cols = lax.ppermute(columns, "sub", ring(2))

    target = (subgrid_id // members * fac_count + w_plane) * members + subgrid_id % members
    packet = pl.pallas_call(
        functools.partial(pack_kernel, capacity, dest_count),
        out_shape=jax.ShapeDtypeStruct((slots, 4 * LANES), jnp.bfloat16),
        in_specs=whole(5),
        out_specs=whole(1)[0],
        compiler_params=params(),
    )(target[None, :], visibility, vis_weight, tap_start, tap_step)
    packet = lax.all_to_all(
        packet.reshape(sub_count * fac_count, members * capacity, 4 * LANES),
        ("sub", "fac"),
        split_axis=0,
        concat_axis=0,
        tiled=True,
    ).reshape(slots, 4 * LANES)
    scaled, position, counts = pl.pallas_call(
        functools.partial(sort_kernel, capacity, members),
        out_shape=(
            jax.ShapeDtypeStruct((slots, 2 * LANES), jnp.float32),
            jax.ShapeDtypeStruct((slots, 2 * LANES), jnp.int32),
            jax.ShapeDtypeStruct((members,), jnp.int32),
        ),
        in_specs=whole(1),
        out_specs=(*whole(2), smem),
        compiler_params=params(),
    )(packet)

    owns, nears, fars = [], [], []
    for m in range(members):
        block = pl.BlockSpec((part, 2 * LANES), lambda i, m=m: (m, 0))
        piece = pl.BlockSpec((2, BAND, SG), lambda i: (0, 0, 0))
        own, near, far = pl.pallas_call(
            functools.partial(grid_kernel, m),
            grid=(1,),
            out_shape=(
                jax.ShapeDtypeStruct((2, BAND, SG), jnp.float32),
                jax.ShapeDtypeStruct((2, BAND, SG), jnp.bfloat16),
                jax.ShapeDtypeStruct((2, BAND, SG), jnp.bfloat16),
            ),
            in_specs=[block, block, smem, smem],
            out_specs=(piece, piece, piece),
            scratch_shapes=[
                pltpu.VMEM((2 * SG, BATCH * LANES), jnp.bfloat16),
                pltpu.VMEM((SG, BATCH * LANES), jnp.bfloat16),
                pltpu.VMEM((2 * SG, SG), jnp.float32),
            ],
            compiler_params=params(),
            cost_estimate=pl.CostEstimate(
                flops=2 * 2 * SG * SG * part * chans, bytes_accessed=2**20, transcendentals=0
            ),
        )(scaled, position, counts, tile_intersection)
        owns.append(own)
        nears.append(lax.ppermute(near, "sub", ring(1)))
        fars.append(lax.ppermute(far, "sub", ring(2)))

    places = jnp.concatenate([columns, next_cols, far_cols])
    high = 16
    cut = pl.BlockSpec((1, high, SG), lambda p, i: (p, i, 0))
    return pl.pallas_call(
        functools.partial(place_kernel, 3 * members),
        grid=(2, BAND // high),
        out_shape=jax.ShapeDtypeStruct((1, 2, BAND, GS), jnp.float32),
        in_specs=[smem] + [cut] * (3 * members),
        out_specs=pl.BlockSpec((1, 1, high, GS), lambda p, i: (0, p, i, 0)),
        compiler_params=params(),
    )(places, *owns, *nears, *fars)


def solution(mesh):
    placed = (
        P(("sub", "fac"), None),
        P(("sub", "fac"), None),
        P(("sub", "fac"), None),
        P(("sub", "fac"), None),
        P(("sub", "fac")),
        P(("sub", "fac")),
        P("sub", None),
    )
    return jax.shard_map(
        shards, mesh=mesh, in_specs=placed, out_specs=P("fac", None, "sub", None), check_vma=False
    )
```

```python
import functools
import math

import jax
import jax.numpy as jnp
from jax import lax
from jax.experimental import pallas as pl
from jax.experimental.pallas import tpu as pltpu
from jax.sharding import PartitionSpec as P

SG = 256
GS = 8192
BAND = 128
LANES = 128
BATCH = 8
VMEM_LIMIT = 48 * 1024 * 1024

kernel_norm = 1.6e-07
SERIES = [kernel_norm * 81.0**k / math.factorial(k) ** 2 for k in range(1, 40)]

NT = (((1,), (1,)), ((), ()))
NN = (((1,), (0,)), ((), ()))


def iota(shape, axis):
    return lax.broadcasted_iota(jnp.int32, shape, axis)


def onehot(mask):
    return jnp.where(mask, 1.0, 0.0).astype(jnp.bfloat16)


def dot(a, b, dims=NN):
    return lax.dot_general(a, b, dims, preferred_element_type=jnp.float32)


def pack_kernel(capacity, dest_count, members, planes, subgrid, plane, vis, weight, start, step, packet):
    rows = vis.shape[0]
    slots = packet.shape[0]
    sub = jnp.floor((subgrid[...].astype(jnp.float32) + 0.5) * (1.0 / members)).astype(jnp.int32)
    goal = (sub * planes + plane[...]) * members + subgrid[...] - sub * members
    named = iota((dest_count, rows), 0) == goal
    ahead = onehot(iota((rows, rows), 0) < iota((rows, rows), 1))
    before = dot(onehot(named), ahead)
    rank = jnp.sum(jnp.where(named, before, 0.0), axis=0, keepdims=True)
    slot = goal * capacity + rank.astype(jnp.int32)
    place = onehot(iota((slots, rows), 0) == slot)
    line = iota((LANES, rows), 0)
    begin, pace = start[...], step[...]
    value = jnp.where(line < 3, begin[0:1], begin[1:2])
    value = jnp.where(line < 6, value, pace[0:1])
    value = jnp.where(line < 8, value, pace[1:2])
    piece = jnp.where(line < 3, line, line - 3)
    piece = jnp.where(line < 6, piece, line - 6)
    piece = jnp.where(line < 8, piece, line - 8)
    piece = jnp.minimum(piece, 3) * 8
    value = jnp.right_shift(value, piece) & 255
    value = jnp.where(line < 10, value, jnp.where(line == 10, 1, 0))
    track = value.astype(jnp.float32).astype(jnp.bfloat16)
    packet[:, 0 : 2 * LANES] = dot(place, vis[...]).astype(jnp.bfloat16)
    packet[:, 2 * LANES : 3 * LANES] = dot(place, weight[...]).astype(jnp.bfloat16)
    packet[:, 3 * LANES : 4 * LANES] = dot(place, track, NT).astype(jnp.bfloat16)


def sort_kernel(capacity, members, packet, scaled, position, counts):
    slots = packet.shape[0]
    part = slots // members
    track = packet[:, 3 * LANES : 4 * LANES]
    used = dot(onehot(iota((8, LANES), 1) == 10), track, NT)[0:1]
    slot = iota((1, slots), 1).astype(jnp.float32)
    group = jnp.floor((slot + 0.5) * (1.0 / capacity))
    cycle = jnp.floor((group + 0.5) * (1.0 / members))
    member = (group - cycle * members).astype(jnp.int32)
    ahead = onehot(iota((slots, slots), 0) < iota((slots, slots), 1))
    mine = (iota((8, slots), 0) == member) & (used > 0.5)
    before = dot(onehot(mine), ahead)
    rank = jnp.sum(jnp.where(mine, before, 0.0), axis=0, keepdims=True).astype(jnp.int32)
    goal = jnp.where(used > 0.5, member * part + rank, -1)
    place = onehot(iota((slots, slots), 0) == goal)
    for m in range(members):
        counts[m] = jnp.sum(jnp.where((member == m) & (used > 0.5), 1, 0))
    weight = dot(place, packet[:, 2 * LANES : 3 * LANES])
    scaled[:, 0:LANES] = dot(place, packet[:, 0:LANES]) * weight
    scaled[:, LANES : 2 * LANES] = dot(place, packet[:, LANES : 2 * LANES]) * weight
    line, chan = iota((LANES, LANES), 0), iota((LANES, LANES), 1)
    moved = dot(place, track).astype(jnp.bfloat16)
    for axis in range(2):
        mix = jnp.zeros((LANES, LANES), jnp.int32)
        for n in range(3):
            mix = jnp.where(line == 3 * axis + n, 256**n, mix)
        for n in range(2):
            mix = jnp.where(line == 6 + 2 * axis + n, chan * 256**n, mix)
        mix = mix.astype(jnp.float32).astype(jnp.bfloat16)
        position[:, axis * LANES : (axis + 1) * LANES] = dot(moved, mix).astype(jnp.int32)


def taps(place):
    shape = (place.shape[0], 8, LANES)
    spot = jnp.broadcast_to(place[:, None, :], shape)
    first = jnp.right_shift(spot, 10) - 3
    cell = first + ((iota(shape, 1) - first) & 7)
    offset = (cell * 1024 - spot).astype(jnp.float32) * (1.0 / 1024.0)
    inside = jnp.maximum(1.0 - offset * offset * 0.0625, 0.0)
    total = jnp.full(shape, SERIES[-1], jnp.float32)
    for term in SERIES[-2::-1]:
        total = total * inside + term
    return total * inside, cell


def halves(cell):
    block = jnp.right_shift(cell, 4)
    upper = (cell & 8) != 0
    low = jnp.where(upper, -1, block)
    high = jnp.where(upper, block, -1)
    return jnp.concatenate([low, high], axis=1).astype(jnp.int16)


def twice(value):
    return jnp.concatenate([value, value], axis=1).astype(jnp.bfloat16)


def grid_kernel(member, scaled, position, counts, corner, own, near, far, left_a, right_a, left_b, right_b, total):
    last = scaled.shape[0] // BATCH - 1

    def build(b, left, right):
        rows = pl.ds(pl.multiple_of(jnp.minimum(b, last) * BATCH, BATCH), BATCH)
        tap_u, cell_u = taps(position[rows, 0:LANES])
        tap_v, cell_v = taps(position[rows, LANES : 2 * LANES])
        block_u, block_v = halves(cell_u), halves(cell_v)
        right_tap = twice(tap_u)
        real = twice(scaled[rows, 0:LANES][:, None, :] * tap_v)
        imag = twice(scaled[rows, LANES : 2 * LANES][:, None, :] * tap_v)
        zero = jnp.zeros((16, LANES), jnp.bfloat16)
        for r in range(BATCH):
            cols = slice(r * LANES, (r + 1) * LANES)
            for k in range(SG // 16):
                here = block_u[r] == jnp.int16(k)
                right[k * 16 : (k + 1) * 16, cols] = jnp.where(here, right_tap[r], zero)
                here = block_v[r] == jnp.int16(k)
                left[k * 16 : (k + 1) * 16, cols] = jnp.where(here, real[r], zero)
                left[SG + k * 16 : SG + (k + 1) * 16, cols] = jnp.where(here, imag[r], zero)

    def pair(i, carry):
        build(2 * i + 1, left_b, right_b)
        total[...] += dot(left_a[...], right_a[...], NT)
        build(2 * i + 2, left_a, right_a)
        total[...] += dot(left_b[...], right_b[...], NT)
        return carry

    total[...] = jnp.zeros_like(total)
    build(0, left_a, right_a)
    lax.fori_loop(0, (counts[member] + 2 * BATCH - 1) // (2 * BATCH), pair, 0)
    shift = corner[member, 0]
    for p in range(2):
        grid = total[p * SG : (p + 1) * SG, :]
        spread = jnp.concatenate([grid, jnp.zeros((BAND, SG), jnp.float32)], axis=0)
        spread = pltpu.roll(spread, shift, 0)
        own[p] = spread[0:BAND]
        near[p] = spread[BAND : 2 * BAND].astype(near.dtype)
        far[p] = spread[2 * BAND :].astype(far.dtype)


def place_kernel(count, columns, *refs):
    band = refs[-1]
    width = band.shape[-1]
    band[...] = jnp.zeros_like(band)
    for n, ref in enumerate(refs[:-1]):
        column = columns[n]
        base = jnp.minimum(lax.shift_right_logical(column, 7), (width - 3 * LANES) // LANES)
        piece = ref[0].astype(jnp.float32)
        piece = jnp.concatenate([piece, jnp.zeros((piece.shape[0], LANES), jnp.float32)], axis=1)
        piece = pltpu.roll(piece, column - base * LANES, 1)
        cols = pl.ds(pl.multiple_of(base * LANES, LANES), 3 * LANES)
        band[0, 0, :, cols] += piece


def params(**extra):
    return pltpu.CompilerParams(vmem_limit_bytes=VMEM_LIMIT, **extra)


def whole(count):
    return [pl.BlockSpec(memory_space=pltpu.VMEM)] * count


def shards(visibility, vis_weight, tap_start, tap_step, subgrid_id, w_plane, tile_intersection):
    sub_count = lax.axis_size("sub")
    fac_count = lax.axis_size("fac")
    rows, chans = vis_weight.shape
    members = tile_intersection.shape[0]
    dest_count = sub_count * fac_count * members
    capacity = max(2, (2 * rows + dest_count - 1) // dest_count)
    slots = dest_count * capacity
    part = slots // members
    smem = pl.BlockSpec(memory_space=pltpu.SMEM)

    columns = tile_intersection[:, 1]
    ring = lambda d: [((i - d) % sub_count, i) for i in range(sub_count)]
    next_cols = lax.ppermute(columns, "sub", ring(1))
    far_cols = lax.ppermute(columns, "sub", ring(2))

    packet = pl.pallas_call(
        functools.partial(pack_kernel, capacity, dest_count, members, fac_count),
        out_shape=jax.ShapeDtypeStruct((slots, 4 * LANES), jnp.bfloat16),
        in_specs=whole(6),
        out_specs=whole(1)[0],
        compiler_params=params(),
    )(subgrid_id[None, :], w_plane[None, :], visibility, vis_weight, tap_start.T, tap_step.T)
    packet = lax.all_to_all(
        packet.reshape(sub_count * fac_count, members * capacity, 4 * LANES),
        ("sub", "fac"),
        split_axis=0,
        concat_axis=0,
        tiled=True,
    ).reshape(slots, 4 * LANES)
    scaled, position, counts = pl.pallas_call(
        functools.partial(sort_kernel, capacity, members),
        out_shape=(
            jax.ShapeDtypeStruct((slots, 2 * LANES), jnp.float32),
            jax.ShapeDtypeStruct((slots, 2 * LANES), jnp.int32),
            jax.ShapeDtypeStruct((members,), jnp.int32),
        ),
        in_specs=whole(1),
        out_specs=(*whole(2), smem),
        compiler_params=params(),
    )(packet)

    owns, nears, fars = [], [], []
    for m in range(members):
        block = pl.BlockSpec((part, 2 * LANES), lambda i, m=m: (m, 0))
        piece = pl.BlockSpec((2, BAND, SG), lambda i: (0, 0, 0))
        own, near, far = pl.pallas_call(
            functools.partial(grid_kernel, m),
            grid=(1,),
            out_shape=(
                jax.ShapeDtypeStruct((2, BAND, SG), jnp.float32),
                jax.ShapeDtypeStruct((2, BAND, SG), jnp.bfloat16),
                jax.ShapeDtypeStruct((2, BAND, SG), jnp.bfloat16),
            ),
            in_specs=[block, block, smem, smem],
            out_specs=(piece, piece, piece),
            scratch_shapes=[
                pltpu.VMEM((2 * SG, BATCH * LANES), jnp.bfloat16),
                pltpu.VMEM((SG, BATCH * LANES), jnp.bfloat16),
                pltpu.VMEM((2 * SG, BATCH * LANES), jnp.bfloat16),
                pltpu.VMEM((SG, BATCH * LANES), jnp.bfloat16),
                pltpu.VMEM((2 * SG, SG), jnp.float32),
            ],
            compiler_params=params(),
            cost_estimate=pl.CostEstimate(flops=1000, bytes_accessed=1000, transcendentals=0),
        )(scaled, position, counts, tile_intersection)
        owns.append(own)
        nears.append(lax.ppermute(near, "sub", ring(1)))
        fars.append(lax.ppermute(far, "sub", ring(2)))

    places = jnp.concatenate([columns, next_cols, far_cols])
    high = 64
    cut = pl.BlockSpec((1, high, SG), lambda p, i: (p, i, 0))
    return pl.pallas_call(
        functools.partial(place_kernel, 3 * members),
        grid=(2, BAND // high),
        out_shape=jax.ShapeDtypeStruct((1, 2, BAND, GS), jnp.float32),
        in_specs=[smem] + [cut] * (3 * members),
        out_specs=pl.BlockSpec((1, 1, high, GS), lambda p, i: (0, p, i, 0)),
        compiler_params=params(),
    )(places, *owns, *nears, *fars)


def solution(mesh):
    placed = (
        P(("sub", "fac"), None),
        P(("sub", "fac"), None),
        P(("sub", "fac"), None),
        P(("sub", "fac"), None),
        P(("sub", "fac")),
        P(("sub", "fac")),
        P("sub", None),
    )
    return jax.shard_map(
        shards, mesh=mesh, in_specs=placed, out_specs=P("fac", None, "sub", None), check_vma=False
    )
```

```python
import functools
import math

import jax
import jax.numpy as jnp
from jax import lax
from jax.experimental import pallas as pl
from jax.experimental.pallas import tpu as pltpu
from jax.sharding import PartitionSpec as P

SG = 256
GS = 8192
BAND = 128
LANES = 128
BATCH = 8
VMEM_LIMIT = 48 * 1024 * 1024
PACK_LIMIT = 63 * 1024 * 1024

kernel_norm = 1.6e-07
SERIES = [kernel_norm * 81.0**k / math.factorial(k) ** 2 for k in range(1, 40)]

NT = (((1,), (1,)), ((), ()))
NN = (((1,), (0,)), ((), ()))


def iota(shape, axis):
    return lax.broadcasted_iota(jnp.int32, shape, axis)


def onehot(mask):
    return jnp.where(mask, 1.0, 0.0).astype(jnp.bfloat16)


def dot(a, b, dims=NN):
    return lax.dot_general(a, b, dims, preferred_element_type=jnp.float32)


def pack_kernel(capacity, dest_count, members, planes, subgrid, plane, vis, weight, start, step, packet):
    rows = vis.shape[0]
    slots = packet.shape[0]
    subgrids, w_planes = subgrid[...].reshape(1, rows), plane[...].reshape(1, rows)
    sub = jnp.floor((subgrids.astype(jnp.float32) + 0.5) * (1.0 / members)).astype(jnp.int32)
    goal = (sub * planes + w_planes) * members + subgrids - sub * members
    named = iota((dest_count, rows), 0) == goal
    ahead = onehot(iota((rows, rows), 0) < iota((rows, rows), 1))
    before = dot(onehot(named), ahead)
    rank = jnp.sum(jnp.where(named, before, 0.0), axis=0, keepdims=True)
    slot = goal * capacity + rank.astype(jnp.int32)
    place = onehot(iota((slots, rows), 0) == slot)
    line = iota((LANES, rows), 0)
    begin, pace = start[...], step[...]
    value = jnp.where(line < 3, begin[0:1], begin[1:2])
    value = jnp.where(line < 6, value, pace[0:1])
    value = jnp.where(line < 8, value, pace[1:2])
    piece = jnp.where(line < 3, line, line - 3)
    piece = jnp.where(line < 6, piece, line - 6)
    piece = jnp.where(line < 8, piece, line - 8)
    piece = jnp.minimum(piece, 3) * 8
    value = jnp.right_shift(value, piece) & 255
    value = jnp.where(line < 10, value, jnp.where(line == 10, 1, 0))
    track = value.astype(jnp.float32).astype(jnp.bfloat16)
    packet[:, 0 : 2 * LANES] = dot(place, vis[...]).astype(jnp.bfloat16)
    packet[:, 2 * LANES : 3 * LANES] = dot(place, weight[...]).astype(jnp.bfloat16)
    packet[:, 3 * LANES : 4 * LANES] = dot(place, track, NT).astype(jnp.bfloat16)


def exchange_kernel(sub_count, fac_count, source, landed, send_sem, recv_sem, own_sem):
    count = sub_count * fac_count
    me = lax.axis_index("sub") * fac_count + lax.axis_index("fac")

    def peer(k):
        other = lax.rem(me + k, count)
        return other, (other // fac_count, lax.rem(other, fac_count))

    barrier = pltpu.get_barrier_semaphore()

    def greet(k, carry):
        pl.semaphore_signal(barrier, inc=1, device_id=peer(k)[1], device_id_type=pl.DeviceIdType.MESH)
        return carry

    lax.fori_loop(1, count, greet, 0)
    own = pltpu.make_async_copy(source.at[me], landed.at[me], own_sem)
    own.start()
    pl.semaphore_wait(barrier, count - 1)

    def transfer(k, block):
        other, where = peer(k)
        return pltpu.make_async_remote_copy(
            src_ref=source.at[other],
            dst_ref=landed.at[block],
            send_sem=send_sem.at[k],
            recv_sem=recv_sem.at[k],
            device_id=where,
            device_id_type=pl.DeviceIdType.MESH,
        )

    def send(k, carry):
        transfer(k, me).start()
        return carry

    def finish(k, carry):
        transfer(k, me).wait_send()
        transfer(k, lax.rem(me + count - k, count)).wait_recv()
        return carry

    lax.fori_loop(1, count, send, 0)
    lax.fori_loop(1, count, finish, 0)
    own.wait()


def sort_kernel(capacity, members, packet, scaled, position, counts):
    slots = packet.shape[0]
    part = slots // members
    track = packet[:, 3 * LANES : 4 * LANES]
    used = dot(onehot(iota((8, LANES), 1) == 10), track, NT)[0:1]
    slot = iota((1, slots), 1).astype(jnp.float32)
    group = jnp.floor((slot + 0.5) * (1.0 / capacity))
    cycle = jnp.floor((group + 0.5) * (1.0 / members))
    member = (group - cycle * members).astype(jnp.int32)
    ahead = onehot(iota((slots, slots), 0) < iota((slots, slots), 1))
    mine = (iota((8, slots), 0) == member) & (used > 0.5)
    before = dot(onehot(mine), ahead)
    rank = jnp.sum(jnp.where(mine, before, 0.0), axis=0, keepdims=True).astype(jnp.int32)
    goal = jnp.where(used > 0.5, member * part + rank, -1)
    place = onehot(iota((slots, slots), 0) == goal)
    for m in range(members):
        counts[m] = jnp.sum(jnp.where((member == m) & (used > 0.5), 1, 0))
    weight = dot(place, packet[:, 2 * LANES : 3 * LANES])
    scaled[:, 0:LANES] = dot(place, packet[:, 0:LANES]) * weight
    scaled[:, LANES : 2 * LANES] = dot(place, packet[:, LANES : 2 * LANES]) * weight
    line, chan = iota((LANES, LANES), 0), iota((LANES, LANES), 1)
    moved = dot(place, track).astype(jnp.bfloat16)
    for axis in range(2):
        mix = jnp.zeros((LANES, LANES), jnp.int32)
        for n in range(3):
            mix = jnp.where(line == 3 * axis + n, 256**n, mix)
        for n in range(2):
            mix = jnp.where(line == 6 + 2 * axis + n, chan * 256**n, mix)
        mix = mix.astype(jnp.float32).astype(jnp.bfloat16)
        position[:, axis * LANES : (axis + 1) * LANES] = dot(moved, mix).astype(jnp.int32)


def taps(place):
    shape = (place.shape[0], 8, LANES)
    spot = jnp.broadcast_to(place[:, None, :], shape)
    first = jnp.right_shift(spot, 10) - 3
    cell = first + ((iota(shape, 1) - first) & 7)
    offset = (cell * 1024 - spot).astype(jnp.float32) * (1.0 / 1024.0)
    inside = jnp.maximum(1.0 - offset * offset * 0.0625, 0.0)
    total = jnp.full(shape, SERIES[-1], jnp.float32)
    for term in SERIES[-2::-1]:
        total = total * inside + term
    return total * inside, cell


def halves(cell):
    block = jnp.right_shift(cell, 4)
    upper = (cell & 8) != 0
    low = jnp.where(upper, -1, block)
    high = jnp.where(upper, block, -1)
    return jnp.concatenate([low, high], axis=1).astype(jnp.int16)


def twice(value):
    return jnp.concatenate([value, value], axis=1).astype(jnp.bfloat16)


def grid_kernel(member, scaled, position, counts, corner, *refs):
    own, near, far, left_a, right_a, left_b, right_b, total = refs[-8:]
    last = scaled.shape[0] // BATCH - 1

    def build(b, left, right):
        rows = pl.ds(pl.multiple_of(jnp.minimum(b, last) * BATCH, BATCH), BATCH)
        tap_u, cell_u = taps(position[rows, 0:LANES])
        tap_v, cell_v = taps(position[rows, LANES : 2 * LANES])
        block_u, block_v = halves(cell_u), halves(cell_v)
        right_tap = twice(tap_u)
        real = twice(scaled[rows, 0:LANES][:, None, :] * tap_v)
        imag = twice(scaled[rows, LANES : 2 * LANES][:, None, :] * tap_v)
        zero = jnp.zeros((16, LANES), jnp.bfloat16)
        for r in range(BATCH):
            cols = slice(r * LANES, (r + 1) * LANES)
            for k in range(SG // 16):
                here = block_u[r] == jnp.int16(k)
                right[k * 16 : (k + 1) * 16, cols] = jnp.where(here, right_tap[r], zero)
                here = block_v[r] == jnp.int16(k)
                left[k * 16 : (k + 1) * 16, cols] = jnp.where(here, real[r], zero)
                left[SG + k * 16 : SG + (k + 1) * 16, cols] = jnp.where(here, imag[r], zero)

    def pair(i, carry):
        build(2 * i + 1, left_b, right_b)
        total[...] += dot(left_a[...], right_a[...], NT)
        build(2 * i + 2, left_a, right_a)
        total[...] += dot(left_b[...], right_b[...], NT)
        return carry

    total[...] = jnp.zeros_like(total)
    build(0, left_a, right_a)
    lax.fori_loop(0, (counts[member] + 2 * BATCH - 1) // (2 * BATCH), pair, 0)
    shift = corner[member, 0]
    for p in range(2):
        grid = total[p * SG : (p + 1) * SG, :]
        spread = jnp.concatenate([grid, jnp.zeros((BAND, SG), jnp.float32)], axis=0)
        spread = pltpu.roll(spread, shift, 0)
        own[p] = spread[0:BAND]
        near[p] = spread[BAND : 2 * BAND].astype(near.dtype)
        far[p] = spread[2 * BAND :].astype(far.dtype)


def place_kernel(count, columns, *refs):
    band = refs[-1]
    width = band.shape[-1]
    band[...] = jnp.zeros_like(band)
    for n, ref in enumerate(refs[:-1]):
        column = columns[n]
        base = jnp.minimum(lax.shift_right_logical(column, 7), (width - 3 * LANES) // LANES)
        piece = ref[0].astype(jnp.float32)
        piece = jnp.concatenate([piece, jnp.zeros((piece.shape[0], LANES), jnp.float32)], axis=1)
        piece = pltpu.roll(piece, column - base * LANES, 1)
        cols = pl.ds(pl.multiple_of(base * LANES, LANES), 3 * LANES)
        band[0, 0, :, cols] += piece


def params(limit=VMEM_LIMIT, **extra):
    return pltpu.CompilerParams(vmem_limit_bytes=limit, **extra)


def whole(count):
    return [pl.BlockSpec(memory_space=pltpu.VMEM)] * count


def shards(visibility, vis_weight, tap_start, tap_step, subgrid_id, w_plane, tile_intersection):
    sub_count = lax.axis_size("sub")
    fac_count = lax.axis_size("fac")
    rows, chans = vis_weight.shape
    members = tile_intersection.shape[0]
    dest_count = sub_count * fac_count * members
    capacity = max(2, (2 * rows + dest_count - 1) // dest_count)
    slots = dest_count * capacity
    part = slots // members
    smem = pl.BlockSpec(memory_space=pltpu.SMEM)

    columns = tile_intersection[:, 1]
    ring = lambda d: [((i - d) % sub_count, i) for i in range(sub_count)]
    next_cols = lax.ppermute(columns, "sub", ring(1))
    far_cols = lax.ppermute(columns, "sub", ring(2))

    packet = pl.pallas_call(
        functools.partial(pack_kernel, capacity, dest_count, members, fac_count),
        out_shape=jax.ShapeDtypeStruct((slots, 4 * LANES), jnp.bfloat16),
        grid=(1,),
        in_specs=[
            pl.BlockSpec((rows,), lambda i: (0,)),
            pl.BlockSpec((rows,), lambda i: (0,)),
            pl.BlockSpec((rows, 2 * chans), lambda i: (0, 0)),
            pl.BlockSpec((rows, chans), lambda i: (0, 0)),
            pl.BlockSpec((2, rows), lambda i: (0, 0)),
            pl.BlockSpec((2, rows), lambda i: (0, 0)),
        ],
        out_specs=pl.BlockSpec((slots, 4 * LANES), lambda i: (0, 0)),
        compiler_params=params(PACK_LIMIT),
    )(subgrid_id, w_plane, visibility, vis_weight, tap_start.T, tap_step.T)
    devices = sub_count * fac_count
    blocks = jax.ShapeDtypeStruct((devices, members * capacity, 4 * LANES), jnp.bfloat16)
    packet = pl.pallas_call(
        functools.partial(exchange_kernel, sub_count, fac_count),
        out_shape=blocks,
        in_specs=[pl.BlockSpec(memory_space=pl.ANY)],
        out_specs=whole(1)[0],
        scratch_shapes=[
            pltpu.SemaphoreType.DMA((devices,)),
            pltpu.SemaphoreType.DMA((devices,)),
            pltpu.SemaphoreType.DMA,
        ],
        compiler_params=params(collective_id=0, has_side_effects=True),
    )(packet.reshape(blocks.shape)).reshape(slots, 4 * LANES)
    scaled, position, counts = pl.pallas_call(
        functools.partial(sort_kernel, capacity, members),
        out_shape=(
            jax.ShapeDtypeStruct((slots, 2 * LANES), jnp.float32),
            jax.ShapeDtypeStruct((slots, 2 * LANES), jnp.int32),
            jax.ShapeDtypeStruct((members,), jnp.int32),
        ),
        in_specs=whole(1),
        out_specs=(*whole(2), smem),
        compiler_params=params(),
    )(packet)

    owns, nears, fars = [], [], []
    for m in range(members):
        arrived = (nears[m - 2], fars[m - 2]) if m >= 2 else (next_cols, far_cols) if m == 1 else ()
        block = pl.BlockSpec((part, 2 * LANES), lambda i, m=m: (m, 0))
        piece = pl.BlockSpec((2, BAND, SG), lambda i: (0, 0, 0))
        own, near, far = pl.pallas_call(
            functools.partial(grid_kernel, m),
            grid=(1,),
            out_shape=(
                jax.ShapeDtypeStruct((2, BAND, SG), jnp.float32),
                jax.ShapeDtypeStruct((2, BAND, SG), jnp.bfloat16),
                jax.ShapeDtypeStruct((2, BAND, SG), jnp.bfloat16),
            ),
            in_specs=[block, block, smem, smem] + [pl.BlockSpec(memory_space=pl.ANY)] * len(arrived),
            out_specs=(piece, piece, piece),
            scratch_shapes=[
                pltpu.VMEM((2 * SG, BATCH * LANES), jnp.bfloat16),
                pltpu.VMEM((SG, BATCH * LANES), jnp.bfloat16),
                pltpu.VMEM((2 * SG, BATCH * LANES), jnp.bfloat16),
                pltpu.VMEM((SG, BATCH * LANES), jnp.bfloat16),
                pltpu.VMEM((2 * SG, SG), jnp.float32),
            ],
            compiler_params=params(),
            cost_estimate=pl.CostEstimate(flops=1000, bytes_accessed=1000, transcendentals=0),
        )(scaled, position, counts, tile_intersection, *arrived)
        owns.append(own)
        nears.append(lax.ppermute(near, "sub", ring(1)))
        fars.append(lax.ppermute(far, "sub", ring(2)))

    places = jnp.concatenate([columns, next_cols, far_cols])
    high = 64
    cut = pl.BlockSpec((1, high, SG), lambda p, i: (p, i, 0))
    return pl.pallas_call(
        functools.partial(place_kernel, 3 * members),
        grid=(2, BAND // high),
        out_shape=jax.ShapeDtypeStruct((1, 2, BAND, GS), jnp.float32),
        in_specs=[smem] + [cut] * (3 * members),
        out_specs=pl.BlockSpec((1, 1, high, GS), lambda p, i: (0, p, i, 0)),
        compiler_params=params(),
    )(places, *owns, *nears, *fars)


def solution(mesh):
    placed = (
        P(("sub", "fac"), None),
        P(("sub", "fac"), None),
        P(("sub", "fac"), None),
        P(("sub", "fac"), None),
        P(("sub", "fac")),
        P(("sub", "fac")),
        P("sub", None),
    )
    return jax.shard_map(
        shards, mesh=mesh, in_specs=placed, out_specs=P("fac", None, "sub", None), check_vma=False
    )
```

```python
import functools
import math

import jax
import jax.numpy as jnp
from jax import lax
from jax.experimental import pallas as pl
from jax.experimental.pallas import tpu as pltpu
from jax.sharding import PartitionSpec as P

SG = 256
GS = 8192
BAND = 128
LANES = 128
BATCH = 8
VMEM_LIMIT = 48 * 1024 * 1024
PACK_LIMIT = 63 * 1024 * 1024

kernel_norm = 1.6e-07
SERIES = [kernel_norm * 81.0**k / math.factorial(k) ** 2 for k in range(1, 40)]

NT = (((1,), (1,)), ((), ()))
NN = (((1,), (0,)), ((), ()))


def iota(shape, axis):
    return lax.broadcasted_iota(jnp.int32, shape, axis)


def onehot(mask):
    return jnp.where(mask, 1.0, 0.0).astype(jnp.bfloat16)


def dot(a, b, dims=NN):
    return lax.dot_general(a, b, dims, preferred_element_type=jnp.float32)


def pack_kernel(capacity, dest_count, members, planes, corner, subgrid, plane, vis, weight, start, step, packet):
    rows = vis.shape[0]
    slots = packet.shape[0]
    subgrids, w_planes = subgrid[...].reshape(1, rows), plane[...].reshape(1, rows)
    sub = jnp.floor((subgrids.astype(jnp.float32) + 0.5) * (1.0 / members)).astype(jnp.int32)
    goal = (sub * planes + w_planes) * members + subgrids - sub * members
    named = iota((dest_count, rows), 0) == goal
    ahead = onehot(iota((rows, rows), 0) < iota((rows, rows), 1))
    before = dot(onehot(named), ahead)
    rank = jnp.sum(jnp.where(named, before, 0.0), axis=0, keepdims=True)
    slot = goal * capacity + rank.astype(jnp.int32)
    place = onehot(iota((slots, rows), 0) == slot)
    line = iota((LANES, rows), 0)
    begin, pace = start[...], step[...]
    value = jnp.where(line < 3, begin[0:1], begin[1:2])
    value = jnp.where(line < 6, value, pace[0:1])
    value = jnp.where(line < 8, value, pace[1:2])
    piece = jnp.where(line < 3, line, line - 3)
    piece = jnp.where(line < 6, piece, line - 6)
    piece = jnp.where(line < 8, piece, line - 8)
    piece = jnp.minimum(piece, 3) * 8
    value = jnp.right_shift(value, piece) & 255
    value = jnp.where(line < 10, value, jnp.where(line == 10, 1, 0))
    track = value.astype(jnp.float32).astype(jnp.bfloat16)
    packet[:, 0 : 2 * LANES] = dot(place, vis[...]).astype(jnp.bfloat16)
    packet[:, 2 * LANES : 3 * LANES] = dot(place, weight[...]).astype(jnp.bfloat16)
    spare = iota((1, LANES), 1)
    columns = jnp.zeros((1, LANES), jnp.int32)
    for m in range(members):
        columns = jnp.where(spare == 11 + 2 * m, corner[m, 1] & 255, columns)
        columns = jnp.where(spare == 12 + 2 * m, lax.shift_right_logical(corner[m, 1], 8), columns)
    packed = dot(place, track, NT) + columns.astype(jnp.float32)
    packet[:, 3 * LANES : 4 * LANES] = packed.astype(jnp.bfloat16)


def exchange_kernel(sub_count, fac_count, source, landed, send_sem, recv_sem, own_sem):
    count = sub_count * fac_count
    me = lax.axis_index("sub") * fac_count + lax.axis_index("fac")

    def peer(k):
        other = lax.rem(me + k, count)
        return other, (other // fac_count, lax.rem(other, fac_count))

    barrier = pltpu.get_barrier_semaphore()

    def greet(k, carry):
        pl.semaphore_signal(barrier, inc=1, device_id=peer(k)[1], device_id_type=pl.DeviceIdType.MESH)
        return carry

    lax.fori_loop(1, count, greet, 0)
    own = pltpu.make_async_copy(source.at[me], landed.at[me], own_sem)
    own.start()
    pl.semaphore_wait(barrier, count - 1)

    def transfer(k, block):
        other, where = peer(k)
        return pltpu.make_async_remote_copy(
            src_ref=source.at[other],
            dst_ref=landed.at[block],
            send_sem=send_sem.at[k],
            recv_sem=recv_sem.at[k],
            device_id=where,
            device_id_type=pl.DeviceIdType.MESH,
        )

    def send(k, carry):
        transfer(k, me).start()
        return carry

    def finish(k, carry):
        transfer(k, me).wait_send()
        transfer(k, lax.rem(me + count - k, count)).wait_recv()
        return carry

    lax.fori_loop(1, count, send, 0)
    lax.fori_loop(1, count, finish, 0)
    own.wait()


def sort_kernel(capacity, members, sub_count, fac_count, packet, scaled, position, counts, places):
    slots = packet.shape[0]
    part = slots // members
    track = packet[:, 3 * LANES : 4 * LANES]
    used = dot(onehot(iota((8, LANES), 1) == 10), track, NT)[0:1]
    slot = iota((1, slots), 1).astype(jnp.float32)
    group = jnp.floor((slot + 0.5) * (1.0 / capacity))
    cycle = jnp.floor((group + 0.5) * (1.0 / members))
    member = (group - cycle * members).astype(jnp.int32)
    ahead = onehot(iota((slots, slots), 0) < iota((slots, slots), 1))
    mine = (iota((8, slots), 0) == member) & (used > 0.5)
    before = dot(onehot(mine), ahead)
    rank = jnp.sum(jnp.where(mine, before, 0.0), axis=0, keepdims=True).astype(jnp.int32)
    goal = jnp.where(used > 0.5, member * part + rank, -1)
    place = onehot(iota((slots, slots), 0) == goal)
    for m in range(members):
        counts[m] = jnp.sum(jnp.where((member == m) & (used > 0.5), 1, 0))
    lane = iota((8, LANES), 1)
    for behind in range(3):
        origin = lax.rem(lax.axis_index("sub") + 2 * sub_count - behind, sub_count) * fac_count
        line = onehot(iota((8, slots), 1) == origin * members * capacity)
        line = jnp.where(iota((8, LANES), 0) == 0, dot(line, track), 0.0).astype(jnp.int32)
        for m in range(members):
            column = jnp.where(lane == 11 + 2 * m, line, jnp.where(lane == 12 + 2 * m, line * 256, 0))
            places[behind * members + m] = jnp.sum(column)
    weight = dot(place, packet[:, 2 * LANES : 3 * LANES])
    scaled[:, 0:LANES] = dot(place, packet[:, 0:LANES]) * weight
    scaled[:, LANES : 2 * LANES] = dot(place, packet[:, LANES : 2 * LANES]) * weight
    line, chan = iota((LANES, LANES), 0), iota((LANES, LANES), 1)
    moved = dot(place, track).astype(jnp.bfloat16)
    for axis in range(2):
        mix = jnp.zeros((LANES, LANES), jnp.int32)
        for n in range(3):
            mix = jnp.where(line == 3 * axis + n, 256**n, mix)
        for n in range(2):
            mix = jnp.where(line == 6 + 2 * axis + n, chan * 256**n, mix)
        mix = mix.astype(jnp.float32).astype(jnp.bfloat16)
        position[:, axis * LANES : (axis + 1) * LANES] = dot(moved, mix).astype(jnp.int32)


def taps(place):
    shape = (place.shape[0], 8, LANES)
    spot = jnp.broadcast_to(place[:, None, :], shape)
    first = jnp.right_shift(spot, 10) - 3
    cell = first + ((iota(shape, 1) - first) & 7)
    offset = (cell * 1024 - spot).astype(jnp.float32) * (1.0 / 1024.0)
    inside = jnp.maximum(1.0 - offset * offset * 0.0625, 0.0)
    total = jnp.full(shape, SERIES[-1], jnp.float32)
    for term in SERIES[-2::-1]:
        total = total * inside + term
    return total * inside, cell


def halves(cell):
    block = jnp.right_shift(cell, 4)
    upper = (cell & 8) != 0
    low = jnp.where(upper, -1, block)
    high = jnp.where(upper, block, -1)
    return jnp.concatenate([low, high], axis=1).astype(jnp.int16)


def twice(value):
    return jnp.concatenate([value, value], axis=1).astype(jnp.bfloat16)


def grid_kernel(member, scaled, position, counts, corner, *refs):
    own, near, far, left_a, right_a, left_b, right_b, total = refs[-8:]
    last = scaled.shape[0] // BATCH - 1

    def build(b, left, right):
        rows = pl.ds(pl.multiple_of(jnp.minimum(b, last) * BATCH, BATCH), BATCH)
        tap_u, cell_u = taps(position[rows, 0:LANES])
        tap_v, cell_v = taps(position[rows, LANES : 2 * LANES])
        block_u, block_v = halves(cell_u), halves(cell_v)
        right_tap = twice(tap_u)
        real = twice(scaled[rows, 0:LANES][:, None, :] * tap_v)
        imag = twice(scaled[rows, LANES : 2 * LANES][:, None, :] * tap_v)
        zero = jnp.zeros((16, LANES), jnp.bfloat16)
        for r in range(BATCH):
            cols = slice(r * LANES, (r + 1) * LANES)
            for k in range(SG // 16):
                here = block_u[r] == jnp.int16(k)
                right[k * 16 : (k + 1) * 16, cols] = jnp.where(here, right_tap[r], zero)
                here = block_v[r] == jnp.int16(k)
                left[k * 16 : (k + 1) * 16, cols] = jnp.where(here, real[r], zero)
                left[SG + k * 16 : SG + (k + 1) * 16, cols] = jnp.where(here, imag[r], zero)

    def pair(i, carry):
        build(2 * i + 1, left_b, right_b)
        total[...] += dot(left_a[...], right_a[...], NT)
        build(2 * i + 2, left_a, right_a)
        total[...] += dot(left_b[...], right_b[...], NT)
        return carry

    total[...] = jnp.zeros_like(total)
    build(0, left_a, right_a)
    lax.fori_loop(0, (counts[member] + 2 * BATCH - 1) // (2 * BATCH), pair, 0)
    shift = corner[member, 0]
    for p in range(2):
        grid = total[p * SG : (p + 1) * SG, :]
        spread = jnp.concatenate([grid, jnp.zeros((BAND, SG), jnp.float32)], axis=0)
        spread = pltpu.roll(spread, shift, 0)
        own[p] = spread[0:BAND]
        near[p] = spread[BAND : 2 * BAND].astype(near.dtype)
        far[p] = spread[2 * BAND :].astype(far.dtype)


def place_kernel(count, columns, *refs):
    band = refs[-1]
    width = band.shape[-1]
    band[...] = jnp.zeros_like(band)
    for n, ref in enumerate(refs[:-1]):
        column = columns[n]
        base = jnp.minimum(lax.shift_right_logical(column, 7), (width - 3 * LANES) // LANES)
        piece = ref[0].astype(jnp.float32)
        piece = jnp.concatenate([piece, jnp.zeros((piece.shape[0], LANES), jnp.float32)], axis=1)
        piece = pltpu.roll(piece, column - base * LANES, 1)
        cols = pl.ds(pl.multiple_of(base * LANES, LANES), 3 * LANES)
        band[0, 0, :, cols] += piece


def params(limit=VMEM_LIMIT, **extra):
    return pltpu.CompilerParams(vmem_limit_bytes=limit, **extra)


def whole(count):
    return [pl.BlockSpec(memory_space=pltpu.VMEM)] * count


def shards(visibility, vis_weight, tap_start, tap_step, subgrid_id, w_plane, tile_intersection):
    sub_count = lax.axis_size("sub")
    fac_count = lax.axis_size("fac")
    rows, chans = vis_weight.shape
    members = tile_intersection.shape[0]
    dest_count = sub_count * fac_count * members
    capacity = max(2, (2 * rows + dest_count - 1) // dest_count)
    slots = dest_count * capacity
    part = slots // members
    smem = pl.BlockSpec(memory_space=pltpu.SMEM)

    ring = lambda d: [((i - d) % sub_count, i) for i in range(sub_count)]
    packet = pl.pallas_call(
        functools.partial(pack_kernel, capacity, dest_count, members, fac_count),
        out_shape=jax.ShapeDtypeStruct((slots, 4 * LANES), jnp.bfloat16),
        grid=(1,),
        in_specs=[
            smem,
            pl.BlockSpec((rows,), lambda i: (0,)),
            pl.BlockSpec((rows,), lambda i: (0,)),
            pl.BlockSpec((rows, 2 * chans), lambda i: (0, 0)),
            pl.BlockSpec((rows, chans), lambda i: (0, 0)),
            pl.BlockSpec((2, rows), lambda i: (0, 0)),
            pl.BlockSpec((2, rows), lambda i: (0, 0)),
        ],
        out_specs=pl.BlockSpec((slots, 4 * LANES), lambda i: (0, 0)),
        compiler_params=params(PACK_LIMIT),
    )(tile_intersection, subgrid_id, w_plane, visibility, vis_weight, tap_start.T, tap_step.T)
    devices = sub_count * fac_count
    blocks = jax.ShapeDtypeStruct((devices, members * capacity, 4 * LANES), jnp.bfloat16)
    packet = pl.pallas_call(
        functools.partial(exchange_kernel, sub_count, fac_count),
        out_shape=blocks,
        in_specs=[pl.BlockSpec(memory_space=pl.ANY)],
        out_specs=whole(1)[0],
        scratch_shapes=[
            pltpu.SemaphoreType.DMA((devices,)),
            pltpu.SemaphoreType.DMA((devices,)),
            pltpu.SemaphoreType.DMA,
        ],
        compiler_params=params(collective_id=0, has_side_effects=True),
    )(packet.reshape(blocks.shape)).reshape(slots, 4 * LANES)
    scaled, position, counts, places = pl.pallas_call(
        functools.partial(sort_kernel, capacity, members, sub_count, fac_count),
        out_shape=(
            jax.ShapeDtypeStruct((slots, 2 * LANES), jnp.float32),
            jax.ShapeDtypeStruct((slots, 2 * LANES), jnp.int32),
            jax.ShapeDtypeStruct((members,), jnp.int32),
            jax.ShapeDtypeStruct((3 * members,), jnp.int32),
        ),
        in_specs=whole(1),
        out_specs=(*whole(2), smem, smem),
        compiler_params=params(),
    )(packet)

    owns, nears, fars = [], [], []
    for m in range(members):
        arrived = (nears[m - 2], fars[m - 2]) if m >= 2 else ()
        block = pl.BlockSpec((part, 2 * LANES), lambda i, m=m: (m, 0))
        piece = pl.BlockSpec((2, BAND, SG), lambda i: (0, 0, 0))
        own, near, far = pl.pallas_call(
            functools.partial(grid_kernel, m),
            grid=(1,),
            out_shape=(
                jax.ShapeDtypeStruct((2, BAND, SG), jnp.float32),
                jax.ShapeDtypeStruct((2, BAND, SG), jnp.bfloat16),
                jax.ShapeDtypeStruct((2, BAND, SG), jnp.bfloat16),
            ),
            in_specs=[block, block, smem, smem] + [pl.BlockSpec(memory_space=pl.ANY)] * len(arrived),
            out_specs=(piece, piece, piece),
            scratch_shapes=[
                pltpu.VMEM((2 * SG, BATCH * LANES), jnp.bfloat16),
                pltpu.VMEM((SG, BATCH * LANES), jnp.bfloat16),
                pltpu.VMEM((2 * SG, BATCH * LANES), jnp.bfloat16),
                pltpu.VMEM((SG, BATCH * LANES), jnp.bfloat16),
                pltpu.VMEM((2 * SG, SG), jnp.float32),
            ],
            compiler_params=params(),
            cost_estimate=pl.CostEstimate(flops=1000, bytes_accessed=1000, transcendentals=0),
        )(scaled, position, counts, tile_intersection, *arrived)
        owns.append(own)
        nears.append(lax.ppermute(near, "sub", ring(1)))
        fars.append(lax.ppermute(far, "sub", ring(2)))

    high = 64
    cut = pl.BlockSpec((1, high, SG), lambda p, i: (p, i, 0))
    return pl.pallas_call(
        functools.partial(place_kernel, 3 * members),
        grid=(2, BAND // high),
        out_shape=jax.ShapeDtypeStruct((1, 2, BAND, GS), jnp.float32),
        in_specs=[smem] + [cut] * (3 * members),
        out_specs=pl.BlockSpec((1, 1, high, GS), lambda p, i: (0, p, i, 0)),
        compiler_params=params(),
    )(places, *owns, *nears, *fars)


def solution(mesh):
    placed = (
        P(("sub", "fac"), None),
        P(("sub", "fac"), None),
        P(("sub", "fac"), None),
        P(("sub", "fac"), None),
        P(("sub", "fac")),
        P(("sub", "fac")),
        P("sub", None),
    )
    return jax.shard_map(
        shards, mesh=mesh, in_specs=placed, out_specs=P("fac", None, "sub", None), check_vma=False
    )
```
